32 devices in a mesh: fsdp: 4 (over y, x), ctx: 4 (over z), tp: 2 (over core).
Axes of the slice: x: 2, y: 2, z: 4, core: 2. Of those that a mesh axis runs over, the one named last changes fastest.
Arguments:
- tokens: bfloat16 [4096, 1024], P(('fsdp', 'ctx'), 'tp'), may hold values from -6 to 6
- w_query: bfloat16 [1024, 1024], P('fsdp', 'tp'), may hold values from -0.1875 to 0.1875
- w_key: bfloat16 [1024, 1024], P('fsdp', 'tp'), may hold values from -0.1875 to 0.1875
- w_value: bfloat16 [1024, 1024], P('fsdp', 'tp'), may hold values from -0.1875 to 0.1875
- w_attn_out: bfloat16 [1024, 1024], P('tp', 'fsdp'), may hold values from -2.5 to 2.5
- w_in: bfloat16 [1024, 4096], P('fsdp', 'tp'), may hold values from -0.1875 to 0.1875
- w_down: bfloat16 [4096, 1024], P('tp', 'fsdp'), may hold values from -0.09375 to 0.09375
- vectors: bfloat16 [8, 1024], P(None, 'tp'), may hold values from -0.4 to 1.4
- bias_in: bfloat16 [4096], P('tp'), may hold values from -0.59765625 to 0.59765625
- lengths: int32 [4], P('fsdp'), may hold values from 256 to 1024, as said below
- cotangent: bfloat16 [4096, 1024], P(('fsdp', 'ctx'), 'tp'), may hold values from -6 to 6
Outputs:
- output: bfloat16 [4096, 1024], P(('fsdp', 'ctx'), 'tp')
- grad_tokens: float32 [4096, 1024], P(('fsdp', 'ctx'), 'tp')
- grad_query: float32 [1024, 1024], P('fsdp', 'tp')
- grad_key: float32 [1024, 1024], P('fsdp', 'tp')
- grad_value: float32 [1024, 1024], P('fsdp', 'tp')
- grad_attn_out: float32 [1024, 1024], P('tp', 'fsdp')
- grad_in: float32 [1024, 4096], P('fsdp', 'tp')
- grad_down: float32 [4096, 1024], P('tp', 'fsdp')
- grad_vectors: float32 [8, 1024], P(None, ('tp', 'fsdp'))
- grad_bias_in: float32 [4096], P(('tp', 'fsdp'))
The draws below stay inside these ranges and needn't reach their ends.
Inputs may be any that keep to these rules, and one draw needn't show every extreme that they name: `lengths`: real positions fill the first slots of a sequence; at least one sequence has 1024.
All inputs are finite; a program needn't handle non-finite values.
Results may differ from the reference program's by a relative error of at most 0.02.
Values may be sent and summed in bfloat16 or wider, within the bound.
A program may use at most 128 MiB of HBM per device.

```python
import jax
import jax.numpy as jnp
from jax import lax

D = 1024
FF = 4096
HEADS = 16
HEAD = 64
SEQ_LEN = 1024
GROUPS = 4
TOKENS = 4096


def draw_vectors(key, part):
    key = jax.random.fold_in(key, 11)
    noise = jnp.clip(jax.random.normal(key, (8, D), jnp.float32), -3.9, 3.9)
    scales = jnp.array([0.1, 0.02, 0.1, 0.1, 0.1, 0.1, 0.1, 0.1], jnp.float32)[:, None]
    centers = jnp.array([0.0, 0.0, 0.0, 0.0, 1.0, 0.0, 1.0, 0.0], jnp.float32)[:, None]
    return (centers + scales * noise).astype(jnp.bfloat16)


def draw_lengths(key, part):
    key = jax.random.fold_in(key, 23)
    first_key, second_key = jax.random.split(key)
    drawn = jax.random.randint(first_key, (GROUPS,), SEQ_LEN // 4, SEQ_LEN + 1)
    chosen = jax.random.randint(second_key, (), 0, GROUPS)
    return jnp.where(jnp.arange(GROUPS) == chosen, SEQ_LEN, drawn).astype(jnp.int32)


def steps_of(own_key, extent, pieces, low, top_value):
    gain, own = 1.0, jax.random.fold_in(own_key, 6)
    for dim, shards_of in pieces:
        heights = jnp.exp(jax.random.uniform(jax.random.fold_in(own, dim), (shards_of,), jnp.float32, low / len(pieces), top_value / len(pieces)))
        gain = gain * jnp.repeat(heights, extent[dim] // shards_of).reshape([-1 if axis == dim else 1 for axis in range(len(extent))])
    return gain


def centred(key, extent, scale, most, shards=(), kind=jnp.bfloat16):
    values = jax.random.normal(key, extent, jnp.float32) * scale
    if len(shards) > 0:
        values = steps_of(key, extent, shards, -0.22, 0.18) * values
    return jnp.clip(values, min=-most, max=most).astype(kind)


def setup_inputs(seed: int = 0) -> dict:
    arg_keys = jax.random.split(jax.random.key(seed), 12)
    return {
        "tokens": centred(arg_keys[0], (TOKENS, D), 1.0, 6.0, ((0, 16), (1, 2))),
        "w_query": centred(arg_keys[1], (D, D), D ** -0.5, 0.1875, ((0, 4), (1, 2))),
        "w_key": centred(arg_keys[2], (D, D), D ** -0.5, 0.1875, ((0, 4), (1, 2))),
        "w_value": centred(arg_keys[3], (D, D), D ** -0.5, 0.1875, ((0, 4), (1, 2))),
        "w_attn_out": centred(arg_keys[4], (D, D), (max(1, 6 * D // SEQ_LEN)) ** -0.5, 2.5, ((0, 2), (1, 4))),
        "w_in": centred(arg_keys[5], (D, FF), D ** -0.5, 0.1875, ((0, 4), (1, 2))),
        "w_down": centred(arg_keys[6], (FF, D), FF ** -0.5, 0.09375, ((0, 2), (1, 4))),
        "vectors": draw_vectors(jax.random.fold_in(arg_keys[11], 71), 0),
        "bias_in": centred(arg_keys[8], (FF,), 0.1, 0.59765625, ((0, 2),)),
        "lengths": draw_lengths(jax.random.fold_in(arg_keys[11], 71), 0),
        "cotangent": centred(arg_keys[10], (TOKENS, D), 1.0, 6.0, ((0, 16), (1, 2))),
    }


norm_eps = 1e-06
masked_score = -1e+30

@jax.custom_vjp
def low(v):
    return lax.optimization_barrier(v.astype(jnp.bfloat16)).astype(jnp.float32)

@jax.custom_vjp
def low_back(v):
    return v

def low_keep(v):
    return (low(v), None)

def low_pass(kept, grad):
    return (grad,)

def back_keep(v):
    return (v, None)

def back_low(kept, grad):
    return (low(grad),)
low.defvjp(low_keep, low_pass)
low_back.defvjp(back_keep, back_low)

def matmul(left_side, right_side):
    return jnp.dot(left_side, right_side, precision=lax.Precision.HIGHEST)

def layer_norm(values_in, gain_row, shift_row):
    center = values_in - lax.optimization_barrier(jnp.mean(values_in, axis=-1, keepdims=True))
    spread = lax.optimization_barrier(jnp.mean(center * center, axis=-1, keepdims=True))
    return center * lax.rsqrt(spread + norm_eps) * gain_row + shift_row

def split_heads(matrix):
    return matrix.reshape(SEQ_LEN, HEADS, HEAD).transpose(1, 0, 2)

def sequence_layer(seq_tokens, seq_length, weights):
    w_q, w_k, w_v, w_o, w_i, w_d, vec_rows, bias_hidden = weights
    key_valid = jnp.arange(SEQ_LEN) < seq_length
    queries = low(low_back(0.125 * (matmul(seq_tokens, w_q) + vec_rows[0])))
    keys_now = low(low_back(matmul(seq_tokens, w_k)))
    values_now = low(low_back(matmul(seq_tokens, w_v) + vec_rows[1]))

    def one_head(triple):
        head_q, head_k, head_v = triple
        scores = low_back(matmul(head_q, head_k.T))
        scores = jnp.where(key_valid[None, :], scores, masked_score)
        top_score = lax.optimization_barrier(jnp.max(scores, axis=-1, keepdims=True))
        weights_exp = jnp.exp(scores - top_score)
        probs = weights_exp / lax.optimization_barrier(jnp.sum(weights_exp, axis=-1, keepdims=True))
        return matmul(low(probs), head_v)
    mixed_heads = lax.map(jax.checkpoint(one_head), (split_heads(queries), split_heads(keys_now), split_heads(values_now)))
    context = low(low_back(mixed_heads.transpose(1, 0, 2).reshape(SEQ_LEN, D)))
    attended = low_back(matmul(context, w_o))
    hidden_one = layer_norm(seq_tokens + attended + vec_rows[2], vec_rows[4], vec_rows[5])
    pre_act = low_back(matmul(low(hidden_one), w_i) + bias_hidden)
    activated = low(jax.nn.gelu(pre_act, approximate=False))
    branch = low_back(matmul(activated, w_d))
    return layer_norm(hidden_one + branch + vec_rows[3], vec_rows[6], vec_rows[7])

def reference(tokens, w_query, w_key, w_value, w_attn_out, w_in, w_down, vectors, bias_in, lengths, cotangent):
    weights = (w_query.astype(jnp.float32), w_key.astype(jnp.float32), w_value.astype(jnp.float32), w_attn_out.astype(jnp.float32), w_in.astype(jnp.float32), w_down.astype(jnp.float32), vectors.astype(jnp.float32), bias_in.astype(jnp.float32))
    token_rows = tokens.astype(jnp.float32)

    def forward(all_tokens, all_weights):
        grouped = all_tokens.reshape(GROUPS, SEQ_LEN, D)

        def per_sequence(pair):
            return sequence_layer(pair[0], pair[1], all_weights)
        outputs = lax.map(jax.checkpoint(per_sequence), (grouped, lengths))
        return outputs.reshape(TOKENS, D)
    layer_out, pull_back = jax.vjp(forward, token_rows, weights)
    row_valid = (jnp.arange(SEQ_LEN)[None, :] < lengths[:, None]).reshape(TOKENS)
    seed_grad = cotangent.astype(jnp.float32) * row_valid[:, None].astype(jnp.float32)
    grad_tokens, grad_weights = pull_back(seed_grad)
    return (layer_out.astype(jnp.bfloat16), grad_tokens, grad_weights[0], grad_weights[1], grad_weights[2], grad_weights[3], grad_weights[4], grad_weights[5], grad_weights[6], grad_weights[7])
```

```python
import functools

import jax
import jax.numpy as jnp
from jax import lax
from jax.experimental import pallas as pl
from jax.experimental.pallas import tpu as pltpu
from jax.sharding import PartitionSpec as P

HEAD = 64
MESH = pl.DeviceIdType.MESH

norm_eps = 1e-06
masked_score = -1e30


def matmul_plain(left_side, right_side):
    return jnp.dot(left_side, right_side, preferred_element_type=jnp.float32)


def matmul_left_t(left_side, right_side):
    return lax.dot_general(
        left_side, right_side, (((0,), (0,)), ((), ())), preferred_element_type=jnp.float32
    )


def matmul_right_t(left_side, right_side):
    return lax.dot_general(
        left_side, right_side, (((1,), (1,)), ((), ())), preferred_element_type=jnp.float32
    )


def norm_forward(values_in, gain_row, shift_row):
    center = values_in - jnp.mean(values_in, axis=-1, keepdims=True)
    spread = jnp.mean(center * center, axis=-1, keepdims=True)
    inv_dev = lax.rsqrt(spread + norm_eps)
    normed = center * inv_dev
    return (normed * gain_row + shift_row, normed, inv_dev)


def norm_backward(grad_out, gain_row, normed, inv_dev):
    grad_normed = grad_out * gain_row
    mean_plain = jnp.mean(grad_normed, axis=-1, keepdims=True)
    mean_normed = jnp.mean(grad_normed * normed, axis=-1, keepdims=True)
    return inv_dev * (grad_normed - mean_plain - normed * mean_normed)


def gelu_exact(values_in):
    return jax.nn.gelu(values_in, approximate=False)


def own_columns(matrix, tp_rank, half_width):
    return lax.dynamic_slice_in_dim(matrix, tp_rank * half_width, half_width, matrix.ndim - 1)


def greet(axis_peers):
    barrier = pltpu.get_barrier_semaphore()
    for peer in axis_peers:
        pl.semaphore_signal(barrier, inc=1, device_id=peer, device_id_type=MESH)
    pl.semaphore_wait(barrier, len(axis_peers))


def remote(src, dst, send_sem, recv_sem, peer):
    return pltpu.make_async_remote_copy(
        src_ref=src,
        dst_ref=dst,
        send_sem=send_sem,
        recv_sem=recv_sem,
        device_id=peer,
        device_id_type=MESH,
    )


def gather_kernel(n, x_ref, out_ref, send_sem, recv_sem, pair_send, pair_recv, own_sem):
    c_rank = lax.axis_index("ctx")
    t_rank = lax.axis_index("tp")
    rows, half = x_ref.shape
    sibling = {"tp": 1 - t_rank}

    def place(c_index, t_index):
        return out_ref.at[
            pl.ds(pl.multiple_of(c_index * rows, rows), rows),
            pl.ds(pl.multiple_of(t_index * half, half), half),
        ]

    greet([{"ctx": lax.rem(c_rank + k, n)} for k in range(1, n)] + [sibling])
    own = place(c_rank, t_rank)
    sends = [
        remote(x_ref, own, send_sem.at[k], recv_sem.at[k], {"ctx": lax.rem(c_rank + k, n)})
        for k in range(1, n)
    ]
    for send in sends:
        send.start()
    pair = [remote(x_ref, own, pair_send.at[0], pair_recv.at[0], sibling)]
    pair[0].start()
    keep = pltpu.make_async_copy(x_ref, own, own_sem)
    keep.start()
    for k in range(1, n):
        spot = place(lax.rem(c_rank + n - k, n), t_rank)
        remote(x_ref, spot, send_sem.at[k], recv_sem.at[k], sibling).wait_recv()
        relay = remote(spot, spot, pair_send.at[k], pair_recv.at[k], sibling)
        relay.start()
        pair.append(relay)
    keep.wait()
    for send in sends:
        send.wait_send()
    for k in range(n):
        pair[k].wait_send()
        spot = place(lax.rem(c_rank + n - k, n), 1 - t_rank)
        remote(x_ref, spot, pair_send.at[k], pair_recv.at[k], sibling).wait_recv()


def gather_rows(own_half, n):
    rows, half = own_half.shape
    return pl.pallas_call(
        functools.partial(gather_kernel, n),
        out_shape=jax.ShapeDtypeStruct((n * rows, 2 * half), own_half.dtype),
        in_specs=[pl.BlockSpec(memory_space=pl.ANY)],
        out_specs=pl.BlockSpec(memory_space=pl.ANY),
        scratch_shapes=[
            pltpu.SemaphoreType.DMA((n,)),
            pltpu.SemaphoreType.DMA((n,)),
            pltpu.SemaphoreType.DMA((n,)),
            pltpu.SemaphoreType.DMA((n,)),
            pltpu.SemaphoreType.DMA,
        ],
        compiler_params=pltpu.CompilerParams(collective_id=0, has_side_effects=True),
        name="gather_rows",
    )(own_half)


def scatter_kernel(
    n,
    share,
    a_ref,
    b_ref,
    out_ref,
    mine,
    give,
    take,
    z_give,
    z_take,
    give_sem,
    take_sem,
    z_give_sem,
    z_take_sem,
    out_sems,
):
    c_rank = lax.axis_index("ctx")
    t_rank = lax.axis_index("tp")
    rows, half = mine.shape[1], mine.shape[2]
    sibling = {"tp": 1 - t_rank}
    greet([{"ctx": lax.rem(c_rank + k, n)} for k in range(1, n)] + [sibling])
    order = list(range(1, n)) + [0]

    def column_part(block, t_index):
        weight = b_ref[pl.ds(pl.multiple_of(t_index * half, half), half), :]
        return matmul_right_t(block, weight)

    pair = {}
    for k in order:
        target = lax.rem(c_rank + k, n)
        block = a_ref[pl.ds(pl.multiple_of(target * rows, rows), rows), :]
        give[k] = column_part(block, 1 - t_rank).astype(give.dtype)
        pair[k] = remote(give.at[k], take.at[k], give_sem.at[k], take_sem.at[k], sibling)
        pair[k].start()
        mine[k] = column_part(block, t_rank)
    sends = {}
    for k in order:
        pair[k].wait_recv()
        if k > 0:
            z_give[k] = (mine[k] + take[k].astype(jnp.float32)).astype(z_give.dtype)
            sends[k] = remote(
                z_give.at[k],
                z_take.at[k],
                z_give_sem.at[k],
                z_take_sem.at[k],
                {"ctx": lax.rem(c_rank + k, n)},
            )
            sends[k].start()
    total = mine[0] + take[0].astype(jnp.float32)
    for k in range(1, n):
        sends[k].wait_recv()
        total = total + z_take[k].astype(jnp.float32)
    if share:
        out_ref[t_rank] = total
        last = remote(
            out_ref.at[t_rank], out_ref.at[t_rank], out_sems.at[0], out_sems.at[1], sibling
        )
        last.start()
        last.wait_send()
        remote(
            out_ref.at[t_rank], out_ref.at[1 - t_rank], out_sems.at[0], out_sems.at[1], sibling
        ).wait_recv()
    else:
        out_ref[0] = total
    for k in order:
        pair[k].wait_send()
    for k in range(1, n):
        sends[k].wait_send()


def scatter_rows(left, right, n, share, kernel_id):
    rows, half = left.shape[0] // n, right.shape[0] // 2
    parts = 2 if share else 1
    blocks = (n, rows, half)
    sem = pltpu.SemaphoreType.DMA((n,))
    return pl.pallas_call(
        functools.partial(scatter_kernel, n, share),
        out_shape=jax.ShapeDtypeStruct((parts, rows, half), jnp.float32),
        in_specs=[pl.BlockSpec(memory_space=pltpu.VMEM)] * 2,
        out_specs=pl.BlockSpec(memory_space=pltpu.VMEM),
        scratch_shapes=[
            pltpu.VMEM(blocks, jnp.float32),
            pltpu.VMEM(blocks, jnp.bfloat16),
            pltpu.VMEM(blocks, jnp.bfloat16),
            pltpu.VMEM(blocks, jnp.bfloat16),
            pltpu.VMEM(blocks, jnp.bfloat16),
            sem,
            sem,
            sem,
            sem,
            pltpu.SemaphoreType.DMA((2,)),
        ],
        compiler_params=pltpu.CompilerParams(
            collective_id=kernel_id, has_side_effects=True, vmem_limit_bytes=40 * 2**20
        ),
        name="scatter_rows",
    )(left, right)


def whole_rows(parts):
    return jnp.concatenate([parts[0], parts[1]], axis=1)


def per_device(
    tokens, w_query, w_key, w_value, w_attn_out, w_in, w_down, vectors, bias_in, lengths, cotangent
):
    row_count, half_width = tokens.shape
    tp_rank = lax.axis_index("tp")
    ctx_rank = lax.axis_index("ctx")
    ctx_size = lax.axis_size("ctx")
    seq_slots = row_count * ctx_size
    head_width = half_width // ctx_size
    heads = head_width // HEAD
    unit_count = w_in.shape[1] // ctx_size

    def own_share(matrix, width, axis):
        return lax.dynamic_slice_in_dim(matrix, ctx_rank * width, width, axis)

    attn_pack = jnp.concatenate(
        [own_share(matrix, head_width, 1) for matrix in (w_query, w_key, w_value)]
        + [own_share(w_attn_out, head_width, 0).T],
        axis=1,
    )
    ffn_pack = jnp.concatenate(
        [own_share(w_in, unit_count, 1), own_share(w_down, unit_count, 0).T], axis=1
    )
    w_attn = lax.all_gather(attn_pack, "fsdp", axis=0, tiled=True)
    w_ffn = lax.all_gather(ffn_pack, "fsdp", axis=0, tiled=True)
    w_qkv, w_o = w_attn[:, : 3 * head_width], w_attn[:, 3 * head_width :]
    w_i, w_d = w_ffn[:, :unit_count], w_ffn[:, unit_count:]

    tok_seq = gather_rows(tokens, ctx_size)
    vec_rows = lax.all_gather(vectors, "tp", axis=1, tiled=True).astype(jnp.float32)
    cot_full = lax.all_gather(cotangent, "tp", axis=1, tiled=True)
    tok_float = lax.dynamic_slice_in_dim(tok_seq, ctx_rank * row_count, row_count, 0).astype(
        jnp.float32
    )
    head_vec = own_share(vectors, head_width, 1).astype(jnp.float32)
    unit_bias = own_share(bias_in, unit_count, 0).astype(jnp.float32)
    seq_length = lengths[0]
    key_valid = jnp.arange(seq_slots) < seq_length
    row_valid = ctx_rank * row_count + jnp.arange(row_count) < seq_length
    seed_grad = cot_full.astype(jnp.float32) * row_valid[:, None].astype(jnp.float32)

    def split_heads(matrix):
        return matrix.reshape(seq_slots, heads, HEAD)

    projected = matmul_plain(tok_seq, w_qkv)
    queries = ((projected[:, :head_width] + head_vec[0]) * 0.125).astype(jnp.bfloat16)
    keys = projected[:, head_width : 2 * head_width].astype(jnp.bfloat16)
    values = (projected[:, 2 * head_width :] + head_vec[1]).astype(jnp.bfloat16)
    head_q, head_k, head_v = split_heads(queries), split_heads(keys), split_heads(values)
    scores = jnp.einsum("qhd,khd->hqk", head_q, head_k, preferred_element_type=jnp.float32)
    scores = jnp.where(key_valid[None, None, :], scores, masked_score)
    top_score = jnp.max(scores, axis=-1, keepdims=True)
    weights_exp = jnp.exp(scores - top_score)
    probs = weights_exp / jnp.sum(weights_exp, axis=-1, keepdims=True)
    probs_low = probs.astype(jnp.bfloat16)
    mixed = jnp.einsum("hqk,khd->qhd", probs_low, head_v, preferred_element_type=jnp.float32)
    context = mixed.reshape(seq_slots, head_width).astype(jnp.bfloat16)

    attended = whole_rows(scatter_rows(context, w_o, ctx_size, True, 1))
    hidden_one, normed_one, inv_one = norm_forward(
        tok_float + attended + vec_rows[2], vec_rows[4], vec_rows[5]
    )
    hidden_seq = gather_rows(
        own_columns(hidden_one, tp_rank, half_width).astype(jnp.bfloat16), ctx_size
    )
    pre_act = matmul_plain(hidden_seq, w_i) + unit_bias
    activated, gelu_pull = jax.vjp(gelu_exact, pre_act)
    act_low = activated.astype(jnp.bfloat16)
    branch = whole_rows(scatter_rows(act_low, w_d, ctx_size, True, 2))
    layer_out, normed_two, inv_two = norm_forward(
        hidden_one + branch + vec_rows[3], vec_rows[6], vec_rows[7]
    )
    output_rows = own_columns(layer_out, tp_rank, half_width).astype(jnp.bfloat16)
    grad_two = norm_backward(seed_grad, vec_rows[6], normed_two, inv_two)
    branch_seq = gather_rows(
        own_columns(grad_two, tp_rank, half_width).astype(jnp.bfloat16), ctx_size
    )
    pre_low = gelu_pull(matmul_plain(branch_seq, w_d))[0].astype(jnp.bfloat16)
    grad_hidden = grad_two + whole_rows(scatter_rows(pre_low, w_i, ctx_size, True, 3))
    grad_one = norm_backward(grad_hidden, vec_rows[4], normed_one, inv_one)
    attn_seq = gather_rows(
        own_columns(grad_one, tp_rank, half_width).astype(jnp.bfloat16), ctx_size
    )

    def share_gradient(pack):
        own_rows = lax.psum_scatter(
            pack.astype(jnp.bfloat16), "fsdp", scatter_dimension=0, tiled=True
        )
        return lax.all_gather(own_rows, "ctx", axis=0).astype(jnp.float32)

    ffn_grads = share_gradient(
        jnp.concatenate(
            [matmul_left_t(hidden_seq, pre_low), matmul_left_t(branch_seq, act_low)], axis=1
        )
    )

    grad_context = matmul_plain(attn_seq, w_o).astype(jnp.bfloat16)
    head_g = split_heads(grad_context)
    grad_probs = jnp.einsum("qhd,khd->hqk", head_g, head_v, preferred_element_type=jnp.float32)
    inner = jnp.sum(probs * grad_probs, axis=-1, keepdims=True)
    grad_scores = (probs * (grad_probs - inner)).astype(jnp.bfloat16)
    grad_q = jnp.einsum("hqk,khd->qhd", grad_scores, head_k, preferred_element_type=jnp.float32)
    grad_k = jnp.einsum("hqk,qhd->khd", grad_scores, head_q, preferred_element_type=jnp.float32)
    grad_v = jnp.einsum("hqk,qhd->khd", probs_low, head_g, preferred_element_type=jnp.float32)
    qkv_low = jnp.concatenate(
        [
            grad_q.reshape(seq_slots, head_width).astype(jnp.bfloat16) * 0.125,
            grad_k.reshape(seq_slots, head_width).astype(jnp.bfloat16),
            grad_v.reshape(seq_slots, head_width).astype(jnp.bfloat16),
        ],
        axis=1,
    )
    attn_grads = share_gradient(
        jnp.concatenate(
            [matmul_left_t(tok_seq, qkv_low), matmul_left_t(attn_seq, context)], axis=1
        )
    )
    grad_tokens = scatter_rows(qkv_low, w_qkv, ctx_size, False, 4)[0] + own_columns(
        grad_one, tp_rank, half_width
    )

    def spread(row, width):
        return lax.dynamic_update_slice_in_dim(
            jnp.zeros((width,), jnp.float32), row, ctx_rank * row.shape[0], 0
        )

    column_sums = jnp.sum(qkv_low.astype(jnp.float32), axis=0)
    small_grads = jnp.concatenate(
        [
            spread(column_sums[:head_width], half_width),
            spread(column_sums[2 * head_width :], half_width),
            own_columns(jnp.sum(grad_one, axis=0), tp_rank, half_width),
            own_columns(jnp.sum(grad_two, axis=0), tp_rank, half_width),
            own_columns(jnp.sum(grad_hidden * normed_one, axis=0), tp_rank, half_width),
            own_columns(jnp.sum(grad_hidden, axis=0), tp_rank, half_width),
            own_columns(jnp.sum(seed_grad * normed_two, axis=0), tp_rank, half_width),
            own_columns(jnp.sum(seed_grad, axis=0), tp_rank, half_width),
            spread(jnp.sum(pre_low.astype(jnp.float32), axis=0), unit_count * ctx_size),
        ]
    )
    small_total = lax.psum(small_grads, ("fsdp", "ctx"))
    fsdp_rank = lax.axis_index("fsdp")
    fsdp_size = lax.axis_size("fsdp")
    vector_grads = own_columns(
        small_total[: 8 * half_width].reshape(8, half_width), fsdp_rank, half_width // fsdp_size
    )
    bias_width = unit_count * ctx_size // fsdp_size
    bias_grad = own_columns(small_total[8 * half_width :], fsdp_rank, bias_width)

    def side_by_side(blocks):
        return blocks.transpose(1, 0, 2).reshape(blocks.shape[1], -1)

    def stacked(blocks):
        return blocks.transpose(0, 2, 1).reshape(-1, blocks.shape[1])

    return (
        output_rows,
        grad_tokens,
        side_by_side(attn_grads[:, :, :head_width]),
        side_by_side(attn_grads[:, :, head_width : 2 * head_width]),
        side_by_side(attn_grads[:, :, 2 * head_width : 3 * head_width]),
        stacked(attn_grads[:, :, 3 * head_width :]),
        side_by_side(ffn_grads[:, :, :unit_count]),
        stacked(ffn_grads[:, :, unit_count:]),
        vector_grads,
        bias_grad,
    )


def solution(mesh):
    placed = (
        P(("fsdp", "ctx"), "tp"),
        P("fsdp", "tp"),
        P("fsdp", "tp"),
        P("fsdp", "tp"),
        P("tp", "fsdp"),
        P("fsdp", "tp"),
        P("tp", "fsdp"),
        P(None, "tp"),
        P("tp"),
        P("fsdp"),
        P(("fsdp", "ctx"), "tp"),
    )
    return jax.shard_map(
        per_device,
        mesh=mesh,
        in_specs=placed,
        out_specs=(
            P(("fsdp", "ctx"), "tp"),
            P(("fsdp", "ctx"), "tp"),
            P("fsdp", "tp"),
            P("fsdp", "tp"),
            P("fsdp", "tp"),
            P("tp", "fsdp"),
            P("fsdp", "tp"),
            P("tp", "fsdp"),
            P(None, ("tp", "fsdp")),
            P(("tp", "fsdp")),
        ),
        check_vma=False,
    )
```

```python
import functools

import jax
import jax.numpy as jnp
from jax import lax
from jax.experimental import pallas as pl
from jax.experimental.pallas import tpu as pltpu
from jax.sharding import PartitionSpec as P

HEAD = 64
MESH = pl.DeviceIdType.MESH

norm_eps = 1e-06
masked_score = -1e30


def matmul_plain(left_side, right_side):
    return jnp.dot(left_side, right_side, preferred_element_type=jnp.float32)


def matmul_left_t(left_side, right_side):
    return lax.dot_general(
        left_side, right_side, (((0,), (0,)), ((), ())), preferred_element_type=jnp.float32
    )


def matmul_right_t(left_side, right_side):
    return lax.dot_general(
        left_side, right_side, (((1,), (1,)), ((), ())), preferred_element_type=jnp.float32
    )


def norm_forward(values_in, gain_row, shift_row):
    center = values_in - jnp.mean(values_in, axis=-1, keepdims=True)
    spread = jnp.mean(center * center, axis=-1, keepdims=True)
    inv_dev = lax.rsqrt(spread + norm_eps)
    normed = center * inv_dev
    return (normed * gain_row + shift_row, normed, inv_dev)


def norm_backward(grad_out, gain_row, normed, inv_dev):
    grad_normed = grad_out * gain_row
    mean_plain = jnp.mean(grad_normed, axis=-1, keepdims=True)
    mean_normed = jnp.mean(grad_normed * normed, axis=-1, keepdims=True)
    return inv_dev * (grad_normed - mean_plain - normed * mean_normed)


def gelu_exact(values_in):
    return jax.nn.gelu(values_in, approximate=False)


def own_columns(matrix, tp_rank, half_width):
    return lax.dynamic_slice_in_dim(matrix, tp_rank * half_width, half_width, matrix.ndim - 1)


def greet(n, axes):
    barrier = pltpu.get_barrier_semaphore()
    c_rank = lax.axis_index("ctx")

    def hail(peer):
        pl.semaphore_signal(barrier, inc=1, device_id=peer, device_id_type=MESH)

    @pl.when(c_rank > 0)
    def _():
        hail({"ctx": c_rank - 1})

    @pl.when(c_rank < n - 1)
    def _():
        hail({"ctx": c_rank + 1})

    hail({"tp": 1 - lax.axis_index("tp")})
    others = 1
    for axis, size in axes:
        for k in range(1, size):
            hail({axis: lax.rem(lax.axis_index(axis) + k, size)})
        others += size - 1
    edge = jnp.where(c_rank > 0, 1, 0) + jnp.where(c_rank < n - 1, 1, 0)
    pl.semaphore_wait(barrier, others + edge)


def remote(src, dst, send_sem, recv_sem, peer):
    return pltpu.make_async_remote_copy(
        src_ref=src,
        dst_ref=dst,
        send_sem=send_sem,
        recv_sem=recv_sem,
        device_id=peer,
        device_id_type=MESH,
    )


def gather_kernel(n, x_ref, out_ref, send_r, recv_r, send_l, recv_l, pair_send, pair_recv, own_sem):
    c_rank = lax.axis_index("ctx")
    t_rank = lax.axis_index("tp")
    rows, half = x_ref.shape
    sibling = {"tp": 1 - t_rank}

    def place(c_index, t_index):
        return out_ref.at[
            pl.ds(pl.multiple_of(c_index * rows, rows), rows),
            pl.ds(pl.multiple_of(t_index * half, half), half),
        ]

    def to_side(step, sign):
        spot = place(c_rank - sign * step, t_rank)
        send, recv = (send_r, recv_r) if sign > 0 else (send_l, recv_l)
        source = x_ref if step == 0 else spot
        return remote(source, spot, send.at[step], recv.at[step], {"ctx": c_rank + sign})

    def from_side(step, sign):
        spot = place(c_rank - sign * (step + 1), t_rank)
        send, recv = (send_r, recv_r) if sign > 0 else (send_l, recv_l)
        return remote(spot, spot, send.at[step], recv.at[step], sibling)

    def sends(step, sign):
        if sign > 0:
            return jnp.logical_and(c_rank - step >= 0, c_rank < n - 1)
        return jnp.logical_and(c_rank + step <= n - 1, c_rank > 0)

    def receives(step, sign):
        return c_rank - 1 - step >= 0 if sign > 0 else c_rank + 1 + step <= n - 1

    def relay(index, t_index):
        spot = place(index, t_index)
        return remote(spot, spot, pair_send.at[index], pair_recv.at[index], sibling)

    greet(n, ())
    for sign in (1, -1):

        @pl.when(sends(0, sign))
        def _(sign=sign):
            to_side(0, sign).start()

    own = place(c_rank, t_rank)
    own_pair = remote(x_ref, own, pair_send.at[c_rank], pair_recv.at[c_rank], sibling)
    own_pair.start()
    keep = pltpu.make_async_copy(x_ref, own, own_sem)
    keep.start()
    for step in range(n - 1):
        for sign in (1, -1):

            @pl.when(receives(step, sign))
            def _(step=step, sign=sign):
                from_side(step, sign).wait_recv()
                if step + 1 < n - 1:

                    @pl.when(sends(step + 1, sign))
                    def _():
                        to_side(step + 1, sign).start()

                relay(c_rank - sign * (step + 1), t_rank).start()

    keep.wait()
    own_pair.wait_send()
    relay(c_rank, 1 - t_rank).wait_recv()
    for step in range(n - 1):
        for sign in (1, -1):

            @pl.when(sends(step, sign))
            def _(step=step, sign=sign):
                to_side(step, sign).wait_send()

            @pl.when(receives(step, sign))
            def _(step=step, sign=sign):
                relay(c_rank - sign * (step + 1), t_rank).wait_send()
                relay(c_rank - sign * (step + 1), 1 - t_rank).wait_recv()


def gather_rows(own_half, n):
    rows, half = own_half.shape
    return pl.pallas_call(
        functools.partial(gather_kernel, n),
        out_shape=jax.ShapeDtypeStruct((n * rows, 2 * half), own_half.dtype),
        in_specs=[pl.BlockSpec(memory_space=pl.ANY)],
        out_specs=pl.BlockSpec(memory_space=pl.ANY),
        scratch_shapes=[
            *[pltpu.SemaphoreType.DMA((n,)) for _ in range(6)],
            pltpu.SemaphoreType.DMA,
        ],
        compiler_params=pltpu.CompilerParams(collective_id=0, has_side_effects=True),
        name="gather_rows",
    )(own_half)


class LineScatter:
    def __init__(self, n, a_ref, b_ref, scratch):
        self.n, self.a_ref, self.b_ref = n, a_ref, b_ref
        self.mine, self.give, self.take, self.z_give, self.z_take = scratch[:5]
        self.give_sem, self.take_sem, self.z_give_sem, self.z_take_sem = scratch[5:9]
        self.c_rank, self.t_rank = lax.axis_index("ctx"), lax.axis_index("tp")

    def column_part(self, block, t_index):
        half = self.mine.shape[2]
        weight = self.b_ref[pl.ds(pl.multiple_of(t_index * half, half), half), :]
        return matmul_right_t(block, weight)

    def pair(self, j):
        return remote(
            self.give.at[j],
            self.take.at[j],
            self.give_sem.at[j],
            self.take_sem.at[j],
            {"tp": 1 - self.t_rank},
        )

    def onward(self, j, sign):
        return remote(
            self.z_give.at[j],
            self.z_take.at[j],
            self.z_give_sem.at[j],
            self.z_take_sem.at[j],
            {"ctx": self.c_rank + sign},
        )

    def onward_last(self, j):
        return remote(
            self.z_give.at[j],
            self.z_take.at[self.n],
            self.z_give_sem.at[j],
            self.z_take_sem.at[self.n],
            {"ctx": self.c_rank - 1},
        )

    def inward(self, slot):
        return remote(
            self.z_take.at[slot],
            self.z_take.at[slot],
            self.z_take_sem.at[slot],
            self.z_take_sem.at[slot],
            {"tp": 1 - self.t_rank},
        )

    def each(self, body):
        for distance in range(self.n - 1, -1, -1):
            for sign in (1, -1) if distance > 0 else (1,):
                j = self.c_rank + sign * distance
                inside = j < self.n if sign > 0 else j >= 0

                @pl.when(inside)
                def _(j=j, sign=sign, distance=distance):
                    body(j, sign, distance)

    def products(self, j, sign, distance):
        rows = self.mine.shape[1]
        block = self.a_ref[pl.ds(pl.multiple_of(j * rows, rows), rows), :]
        self.give[j] = self.column_part(block, 1 - self.t_rank).astype(self.give.dtype)
        self.pair(j).start()
        self.mine[j] = self.column_part(block, self.t_rank)

    def add_inward(self, j, slot):
        self.inward(slot).wait_recv()
        self.mine[j] += self.z_take[slot].astype(jnp.float32)

    def passing(self, j, sign, distance):
        self.pair(j).wait_recv()
        self.mine[j] += self.take[j].astype(jnp.float32)
        behind = self.c_rank > 0 if sign > 0 else self.c_rank < self.n - 1

        @pl.when(behind)
        def _():
            self.add_inward(j, j)

        if distance == 0:

            @pl.when(self.c_rank < self.n - 1)
            def _():
                self.add_inward(j, self.n)

            return
        self.z_give[j] = self.mine[j].astype(self.z_give.dtype)
        if sign < 0 and distance == 1:
            self.onward_last(j).start()
        else:
            self.onward(j, sign).start()

    def ending(self, j, sign, distance):
        self.pair(j).wait_send()
        if distance > 0:
            self.onward(j, sign).wait_send()


def scatter_kernel(n, parts, a_ref, b_ref, *rest):
    fsdp_size = parts
    if fsdp_size:
        pack_ref, out_ref, taken_ref = rest[:3]
        rest = rest[3:]
        f_send, f_recv = rest[10:]
    else:
        out_ref, rest = rest[0], rest[1:]
    out_sems = rest[9]
    t_rank = lax.axis_index("tp")
    sibling = {"tp": 1 - t_rank}
    greet(n, (("fsdp", fsdp_size),) if fsdp_size else ())
    moves = []
    if fsdp_size:
        f_rank = lax.axis_index("fsdp")
        for k in range(1, fsdp_size):
            peer = lax.rem(f_rank + k, fsdp_size)
            moves.append(
                remote(
                    pack_ref.at[peer],
                    taken_ref.at[k - 1],
                    f_send.at[k],
                    f_recv.at[k],
                    {"fsdp": peer},
                )
            )
            moves[-1].start()
    line = LineScatter(n, a_ref, b_ref, rest)
    line.each(line.products)
    line.each(line.passing)
    out_ref[t_rank] = line.mine[line.c_rank]
    last = remote(out_ref.at[t_rank], out_ref.at[t_rank], out_sems.at[0], out_sems.at[1], sibling)
    last.start()
    last.wait_send()
    remote(
        out_ref.at[t_rank], out_ref.at[1 - t_rank], out_sems.at[0], out_sems.at[1], sibling
    ).wait_recv()
    line.each(line.ending)
    for move in moves:
        move.wait_recv()
        move.wait_send()


def line_scratch(n, rows, half):
    sem = pltpu.SemaphoreType.DMA((n + 1,))
    low = pltpu.VMEM((n, rows, half), jnp.bfloat16)
    return [
        pltpu.VMEM((n, rows, half), jnp.float32),
        low,
        low,
        low,
        pltpu.VMEM((n + 1, rows, half), jnp.bfloat16),
        sem,
        sem,
        sem,
        sem,
    ]


IN_VMEM = pl.BlockSpec(memory_space=pltpu.VMEM)
ANYWHERE = pl.BlockSpec(memory_space=pl.ANY)


def scatter_rows(left, right, n, kernel_id, pack=None):
    rows, half = left.shape[0] // n, right.shape[0] // 2
    out_shape = [jax.ShapeDtypeStruct((2, rows, half), jnp.float32)]
    parts = 0
    scratch = line_scratch(n, rows, half) + [pltpu.SemaphoreType.DMA((2,))]
    if pack is not None:
        parts = pack.shape[0]
        out_shape.append(jax.ShapeDtypeStruct((parts - 1,) + pack.shape[1:], pack.dtype))
        scratch += [pltpu.SemaphoreType.DMA((parts,)), pltpu.SemaphoreType.DMA((parts,))]
    extra = () if pack is None else (pack,)
    return pl.pallas_call(
        functools.partial(scatter_kernel, n, parts),
        out_shape=out_shape,
        in_specs=[IN_VMEM, IN_VMEM] + [ANYWHERE] * len(extra),
        out_specs=[IN_VMEM] + [ANYWHERE] * len(extra),
        scratch_shapes=scratch,
        compiler_params=pltpu.CompilerParams(
            collective_id=kernel_id, has_side_effects=True, vmem_limit_bytes=40 * 2**20
        ),
        name="scatter_rows",
    )(left, right, *extra)


def finish_kernel(n, parts, a_ref, b_ref, pack_ref, small_ref, tok_ref, grads_ref, total_ref, *rest):
    f_take, sf_take, sc_give, sc_take = rest[9:13]
    f_send, f_recv, sf_send, sf_recv, g_send, g_recv, sc_send, sc_recv = rest[13:]
    c_rank, f_rank = lax.axis_index("ctx"), lax.axis_index("fsdp")
    greet(n, (("fsdp", parts), ("ctx", n)))
    first, second = [], []
    for k in range(1, parts):
        peer = lax.rem(f_rank + k, parts)
        at = {"fsdp": peer}
        first.append(remote(pack_ref.at[peer], f_take.at[k], f_send.at[k], f_recv.at[k], at))
        first.append(remote(small_ref, sf_take.at[k], sf_send.at[k], sf_recv.at[k], at))
    for move in first:
        move.start()
    line = LineScatter(n, a_ref, b_ref, rest)
    line.each(line.products)
    total = pack_ref[f_rank].astype(jnp.float32)
    small = small_ref[...]
    for k in range(1, parts):
        first[2 * k - 2].wait_recv()
        first[2 * k - 1].wait_recv()
        total = total + f_take[k].astype(jnp.float32)
        small = small + sf_take[k]
    grads_ref[c_rank] = total.astype(grads_ref.dtype)
    sc_give[...] = small
    for k in range(1, n):
        peer = lax.rem(c_rank + k, n)
        at = {"ctx": peer}
        own = grads_ref.at[c_rank]
        second.append(remote(own, own, g_send.at[k], g_recv.at[k], at))
        second.append(remote(sc_give, sc_take.at[k], sc_send.at[k], sc_recv.at[k], at))
    line.each(line.passing)
    for move in second:
        move.start()
    tok_ref[...] = line.mine[c_rank]
    for k in range(1, n):
        spot = grads_ref.at[lax.rem(c_rank + n - k, n)]
        remote(spot, spot, g_send.at[k], g_recv.at[k], {"ctx": lax.rem(c_rank + k, n)}).wait_recv()
        second[2 * k - 1].wait_recv()
        small = small + sc_take[k]
    total_ref[...] = small
    line.each(line.ending)
    for move in first + second:
        move.wait_send()


def finish(left, right, pack, small, n, kernel_id):
    rows, half = left.shape[0] // n, right.shape[0] // 2
    parts = pack.shape[0]
    f_sem, c_sem = pltpu.SemaphoreType.DMA((parts,)), pltpu.SemaphoreType.DMA((n,))
    return pl.pallas_call(
        functools.partial(finish_kernel, n, parts),
        out_shape=[
            jax.ShapeDtypeStruct((rows, half), jnp.float32),
            jax.ShapeDtypeStruct((n,) + pack.shape[1:], pack.dtype),
            jax.ShapeDtypeStruct(small.shape, jnp.float32),
        ],
        in_specs=[IN_VMEM] * 4,
        out_specs=[IN_VMEM] * 3,
        scratch_shapes=line_scratch(n, rows, half)
        + [
            pltpu.VMEM(pack.shape, pack.dtype),
            pltpu.VMEM((parts,) + small.shape, jnp.float32),
            pltpu.VMEM(small.shape, jnp.float32),
            pltpu.VMEM((n,) + small.shape, jnp.float32),
        ]
        + [f_sem] * 4
        + [c_sem] * 4,
        compiler_params=pltpu.CompilerParams(
            collective_id=kernel_id, has_side_effects=True, vmem_limit_bytes=40 * 2**20
        ),
        name="finish",
    )(left, right, pack, small)


def whole_rows(parts):
    return jnp.concatenate([parts[0], parts[1]], axis=1)


def per_device(
    tokens, w_query, w_key, w_value, w_attn_out, w_in, w_down, vectors, bias_in, lengths, cotangent
):
    row_count, half_width = tokens.shape
    tp_rank = lax.axis_index("tp")
    ctx_rank = lax.axis_index("ctx")
    ctx_size = lax.axis_size("ctx")
    seq_slots = row_count * ctx_size
    head_width = half_width // ctx_size
    heads = head_width // HEAD
    unit_count = w_in.shape[1] // ctx_size

    def own_share(matrix, width, axis):
        return lax.dynamic_slice_in_dim(matrix, ctx_rank * width, width, axis)

    attn_pack = jnp.concatenate(
        [own_share(matrix, head_width, 1) for matrix in (w_query, w_key, w_value)]
        + [own_share(w_attn_out, head_width, 0).T],
        axis=1,
    )
    ffn_pack = jnp.concatenate(
        [own_share(w_in, unit_count, 1), own_share(w_down, unit_count, 0).T], axis=1
    )
    w_attn = lax.all_gather(attn_pack, "fsdp", axis=0, tiled=True)
    w_ffn = lax.all_gather(ffn_pack, "fsdp", axis=0, tiled=True)
    w_qkv, w_o = w_attn[:, : 3 * head_width], w_attn[:, 3 * head_width :]
    w_i, w_d = w_ffn[:, :unit_count], w_ffn[:, unit_count:]

    tok_seq = gather_rows(tokens, ctx_size)
    vec_rows = lax.all_gather(vectors, "tp", axis=1, tiled=True).astype(jnp.float32)
    cot_full = lax.all_gather(cotangent, "tp", axis=1, tiled=True)
    tok_float = lax.dynamic_slice_in_dim(tok_seq, ctx_rank * row_count, row_count, 0).astype(
        jnp.float32
    )
    head_vec = own_share(vectors, head_width, 1).astype(jnp.float32)
    unit_bias = own_share(bias_in, unit_count, 0).astype(jnp.float32)
    seq_length = lengths[0]
    key_valid = jnp.arange(seq_slots) < seq_length
    row_valid = ctx_rank * row_count + jnp.arange(row_count) < seq_length
    seed_grad = cot_full.astype(jnp.float32) * row_valid[:, None].astype(jnp.float32)

    def split_heads(matrix):
        return matrix.reshape(seq_slots, heads, HEAD)

    projected = matmul_plain(tok_seq, w_qkv)
    queries = ((projected[:, :head_width] + head_vec[0]) * 0.125).astype(jnp.bfloat16)
    keys = projected[:, head_width : 2 * head_width].astype(jnp.bfloat16)
    values = (projected[:, 2 * head_width :] + head_vec[1]).astype(jnp.bfloat16)
    head_q, head_k, head_v = split_heads(queries), split_heads(keys), split_heads(values)
    scores = jnp.einsum("qhd,khd->hqk", head_q, head_k, preferred_element_type=jnp.float32)
    scores = jnp.where(key_valid[None, None, :], scores, masked_score)
    top_score = jnp.max(scores, axis=-1, keepdims=True)
    weights_exp = jnp.exp(scores - top_score)
    probs = weights_exp / jnp.sum(weights_exp, axis=-1, keepdims=True)
    probs_low = probs.astype(jnp.bfloat16)
    mixed = jnp.einsum("hqk,khd->qhd", probs_low, head_v, preferred_element_type=jnp.float32)
    context = mixed.reshape(seq_slots, head_width).astype(jnp.bfloat16)

    attended = whole_rows(scatter_rows(context, w_o, ctx_size, 1)[0])
    hidden_one, normed_one, inv_one = norm_forward(
        tok_float + attended + vec_rows[2], vec_rows[4], vec_rows[5]
    )
    hidden_seq = gather_rows(
        own_columns(hidden_one, tp_rank, half_width).astype(jnp.bfloat16), ctx_size
    )
    pre_act = matmul_plain(hidden_seq, w_i) + unit_bias
    activated, gelu_pull = jax.vjp(gelu_exact, pre_act)
    act_low = activated.astype(jnp.bfloat16)
    branch = whole_rows(scatter_rows(act_low, w_d, ctx_size, 2)[0])
    layer_out, normed_two, inv_two = norm_forward(
        hidden_one + branch + vec_rows[3], vec_rows[6], vec_rows[7]
    )
    output_rows = own_columns(layer_out, tp_rank, half_width).astype(jnp.bfloat16)
    grad_two = norm_backward(seed_grad, vec_rows[6], normed_two, inv_two)
    branch_seq = gather_rows(
        own_columns(grad_two, tp_rank, half_width).astype(jnp.bfloat16), ctx_size
    )
    pre_low = gelu_pull(matmul_plain(branch_seq, w_d))[0].astype(jnp.bfloat16)
    fsdp_rank = lax.axis_index("fsdp")
    fsdp_size = lax.axis_size("fsdp")

    def fsdp_blocks(*grads):
        pack = jnp.concatenate([grad.astype(jnp.bfloat16) for grad in grads], axis=1)
        return pack.reshape(fsdp_size, -1, pack.shape[1])

    ffn_parts = fsdp_blocks(
        matmul_left_t(hidden_seq, pre_low), matmul_left_t(branch_seq, act_low)
    )
    hidden_parts, ffn_taken = scatter_rows(pre_low, w_i, ctx_size, 3, ffn_parts)
    ffn_own = (
        lax.dynamic_index_in_dim(ffn_parts, fsdp_rank, 0, False).astype(jnp.float32)
        + jnp.sum(ffn_taken.astype(jnp.float32), axis=0)
    ).astype(jnp.bfloat16)
    ffn_grads = lax.all_gather(ffn_own, "ctx", axis=0).astype(jnp.float32)
    grad_hidden = grad_two + whole_rows(hidden_parts)
    grad_one = norm_backward(grad_hidden, vec_rows[4], normed_one, inv_one)
    attn_seq = gather_rows(
        own_columns(grad_one, tp_rank, half_width).astype(jnp.bfloat16), ctx_size
    )

    grad_context = matmul_plain(attn_seq, w_o).astype(jnp.bfloat16)
    head_g = split_heads(grad_context)
    grad_probs = jnp.einsum("qhd,khd->hqk", head_g, head_v, preferred_element_type=jnp.float32)
    inner = jnp.sum(probs * grad_probs, axis=-1, keepdims=True)
    grad_scores = (probs * (grad_probs - inner)).astype(jnp.bfloat16)
    grad_q = jnp.einsum("hqk,khd->qhd", grad_scores, head_k, preferred_element_type=jnp.float32)
    grad_k = jnp.einsum("hqk,qhd->khd", grad_scores, head_q, preferred_element_type=jnp.float32)
    grad_v = jnp.einsum("hqk,qhd->khd", probs_low, head_g, preferred_element_type=jnp.float32)
    qkv_low = jnp.concatenate(
        [
            grad_q.reshape(seq_slots, head_width).astype(jnp.bfloat16) * 0.125,
            grad_k.reshape(seq_slots, head_width).astype(jnp.bfloat16),
            grad_v.reshape(seq_slots, head_width).astype(jnp.bfloat16),
        ],
        axis=1,
    )
    def spread(row, width):
        return lax.dynamic_update_slice_in_dim(
            jnp.zeros((width,), jnp.float32), row, ctx_rank * row.shape[0], 0
        )

    column_sums = jnp.sum(qkv_low.astype(jnp.float32), axis=0)
    small_grads = jnp.concatenate(
        [
            spread(column_sums[:head_width], half_width),
            spread(column_sums[2 * head_width :], half_width),
            own_columns(jnp.sum(grad_one, axis=0), tp_rank, half_width),
            own_columns(jnp.sum(grad_two, axis=0), tp_rank, half_width),
            own_columns(jnp.sum(grad_hidden * normed_one, axis=0), tp_rank, half_width),
            own_columns(jnp.sum(grad_hidden, axis=0), tp_rank, half_width),
            own_columns(jnp.sum(seed_grad * normed_two, axis=0), tp_rank, half_width),
            own_columns(jnp.sum(seed_grad, axis=0), tp_rank, half_width),
            spread(jnp.sum(pre_low.astype(jnp.float32), axis=0), unit_count * ctx_size),
        ]
    )
    attn_parts = fsdp_blocks(matmul_left_t(tok_seq, qkv_low), matmul_left_t(attn_seq, context))
    grad_rows, attn_grads, small_total = finish(
        qkv_low, w_qkv, attn_parts, small_grads.reshape(-1, 128), ctx_size, 4
    )
    grad_tokens = grad_rows + own_columns(grad_one, tp_rank, half_width)
    attn_grads = attn_grads.astype(jnp.float32)
    small_total = small_total.reshape(-1)
    vector_grads = own_columns(
        small_total[: 8 * half_width].reshape(8, half_width), fsdp_rank, half_width // fsdp_size
    )
    bias_width = unit_count * ctx_size // fsdp_size
    bias_grad = own_columns(small_total[8 * half_width :], fsdp_rank, bias_width)

    def side_by_side(blocks):
        return blocks.transpose(1, 0, 2).reshape(blocks.shape[1], -1)

    def stacked(blocks):
        return blocks.transpose(0, 2, 1).reshape(-1, blocks.shape[1])

    return (
        output_rows,
        grad_tokens,
        side_by_side(attn_grads[:, :, :head_width]),
        side_by_side(attn_grads[:, :, head_width : 2 * head_width]),
        side_by_side(attn_grads[:, :, 2 * head_width : 3 * head_width]),
        stacked(attn_grads[:, :, 3 * head_width :]),
        side_by_side(ffn_grads[:, :, :unit_count]),
        stacked(ffn_grads[:, :, unit_count:]),
        vector_grads,
        bias_grad,
    )


def solution(mesh):
    placed = (
        P(("fsdp", "ctx"), "tp"),
        P("fsdp", "tp"),
        P("fsdp", "tp"),
        P("fsdp", "tp"),
        P("tp", "fsdp"),
        P("fsdp", "tp"),
        P("tp", "fsdp"),
        P(None, "tp"),
        P("tp"),
        P("fsdp"),
        P(("fsdp", "ctx"), "tp"),
    )
    return jax.shard_map(
        per_device,
        mesh=mesh,
        in_specs=placed,
        out_specs=(
            P(("fsdp", "ctx"), "tp"),
            P(("fsdp", "ctx"), "tp"),
            P("fsdp", "tp"),
            P("fsdp", "tp"),
            P("fsdp", "tp"),
            P("tp", "fsdp"),
            P("fsdp", "tp"),
            P("tp", "fsdp"),
            P(None, ("tp", "fsdp")),
            P(("tp", "fsdp")),
        ),
        check_vma=False,
    )
```
